256 devices in a mesh: tm: 4 (over z_lo, core), band: 64 (over y, z_hi, x).
Axes of the slice: x: 4, y: 4, z: 8 (z_hi: 4, z_lo: 2; z = z_hi * 2 + z_lo), core: 2. Of those that a mesh axis runs over, the one named last changes fastest.
Arguments:
- volts: bfloat16 [2, 1024, 262144], P(None, 'band', 'tm'), may hold values from -4 to 4
- taps: float32 [8, 256], replicated, may hold values from -2 to 2
Outputs:
- visibilities: float32 [256, 2, 1024, 1024], P(('tm', 'band'))
The draws below stay inside these ranges and needn't reach their ends.
All inputs are finite; a program needn't handle non-finite values.
Results may differ from the reference program's by a relative error of at most 0.0046.
Values may be sent and summed in bfloat16 or wider, within the bound.
No kernel may reach another device: no remote copies, remote signals or barrier semaphores. Data moves between devices by JAX's collectives and lax.ppermute only.
A program may use at most 128 MiB of HBM per device.

```python
import math
import jax
import jax.numpy as jnp
from jax import lax

INPUTS = 1024
CHANNELS = 256
TAPS = 8
SPECTRA = 1024
SAMPLES = 262144


def block_levels(rng, dims, shards, low, high):
    def one(axis_at, blocks):
        steps = jax.random.uniform(jax.random.fold_in(jax.random.fold_in(rng, 6), axis_at), (blocks,), jnp.float32, low / len(shards), high / len(shards))
        return jnp.repeat(jnp.exp(steps), dims[axis_at] // blocks).reshape((-1,) + (1,) * (len(dims) - axis_at - 1))

    gain = one(*shards[0])
    for cut in shards[1:]:
        gain = gain * one(*cut)
    return gain


def bell_draw(own_key, dims, width, reach, cuts=(), kind=jnp.bfloat16):
    array = jax.random.normal(own_key, dims, jnp.float32) * width
    if len(cuts) > 0:
        array = block_levels(own_key, dims, cuts, -0.22, 0.18) * array
    return jnp.clip(array, min=-reach, max=reach).astype(kind)


def setup_inputs(seed: int = 0) -> dict:
    keys = jax.random.split(jax.random.key(seed), 3)
    volts = bell_draw(keys[0], (2, INPUTS, SAMPLES), 1.0, 4.0, ((1, 64), (2, 4)))
    taps = bell_draw(keys[1], (TAPS, CHANNELS), 0.5, 2.0, (), jnp.float32)
    return {"volts": volts, "taps": taps}


def dft_table():
    index = jnp.arange(CHANNELS, dtype=jnp.int32)
    turns = index[:, None] * index[None, :] % CHANNELS
    theta = turns.astype(jnp.float32) * (2.0 * math.pi / CHANNELS)
    factor = 1.0 / math.sqrt(CHANNELS)
    cosine = jnp.cos(theta) * factor
    sine = jnp.sin(theta) * factor
    real_row = jnp.stack([cosine, sine], axis=1)
    imag_row = jnp.stack([-sine, cosine], axis=1)
    table = jnp.stack([real_row, imag_row], axis=1)
    return table.reshape(2 * CHANNELS, 2, CHANNELS).astype(jnp.bfloat16)

def block_spectra(group_volts, taps, table):
    count = group_volts.shape[1]
    leading = jnp.zeros((2, count, (TAPS - 1) * CHANNELS), group_volts.dtype)
    frames = jnp.concatenate([leading, group_volts], axis=2)
    frames = frames.reshape(2, count, SPECTRA + TAPS - 1, CHANNELS).astype(jnp.float32)
    filtered = taps[0] * frames[:, :, 0:SPECTRA, :]
    for weight_index in range(1, TAPS):
        filtered = filtered + taps[weight_index] * frames[:, :, weight_index:weight_index + SPECTRA, :]
    filtered = filtered.astype(jnp.bfloat16)
    spectra = jnp.einsum('mrk,rnsk->mns', table.astype(jnp.float32), filtered.astype(jnp.float32), precision=lax.Precision.HIGHEST)
    return spectra.astype(jnp.bfloat16).reshape(CHANNELS, 2, count, SPECTRA)

def one_channel(signal):
    signal = signal.astype(jnp.float32)
    swapped = jnp.stack([signal[1], -signal[0]])
    weight = jnp.stack([signal, swapped])
    products = jnp.einsum('orps,rqs->opq', weight, signal, precision=lax.Precision.HIGHEST)
    return products * (1.0 / SPECTRA)

def reference(volts, taps):
    table = dft_table()
    group_size = 64
    grouped = volts.reshape(2, INPUTS // group_size, group_size, SAMPLES).transpose(1, 0, 2, 3)
    per_group = lax.map(lambda group_volts: block_spectra(group_volts, taps, table), grouped)
    spectra = per_group.transpose(1, 2, 0, 3, 4).reshape(CHANNELS, 2, INPUTS, SPECTRA)
    return lax.map(one_channel, spectra)
```

```python
import functools
import math

import jax
import jax.numpy as jnp
import ml_dtypes
import numpy as np
from jax import lax
from jax.experimental import pallas as pl
from jax.experimental.pallas import tpu as pltpu
from jax.sharding import PartitionSpec as P

LANES = 128
VMEM_BYTES = 56 * 1024 * 1024


def shifted(shard, axis, by):
    size = lax.axis_size(axis)
    pairs = [(i, i + by) for i in range(size) if 0 <= i + by < size]
    return lax.ppermute(shard, axis, pairs)


def dft_table(channels):
    index = np.arange(channels)
    theta = (index[:, None] * index[None, :] % channels) * (2.0 * math.pi / channels)
    factor = 1.0 / math.sqrt(channels)
    cosine = np.cos(theta) * factor
    sine = np.sin(theta) * factor
    real_row = np.stack([cosine, sine], axis=1)
    imag_row = np.stack([-sine, cosine], axis=1)
    table = np.stack([real_row, imag_row], axis=1)
    return table.reshape(2 * channels, 2 * channels).astype(np.float32).astype(ml_dtypes.bfloat16)


def channelize_kernel(volts_ref, history_ref, taps_ref, table_ref, out_ref, tail, rows, turned):
    taps_count, channels = taps_ref.shape
    inputs = volts_ref.shape[1]
    block = volts_ref.shape[2] // channels
    margin = taps_count - 1

    @pl.when(pl.program_id(0) == 0)
    def _():
        tail[...] = history_ref[...]

    for part in range(2):
        for left in range(0, channels, LANES):
            weights = [taps_ref[j : j + 1, left : left + LANES] for j in range(taps_count)]

            def frame(index):
                if index < margin:
                    at = index * channels + left
                    return tail[part, :, at : at + LANES].astype(jnp.float32)
                at = (index - margin) * channels + left
                return volts_ref[part, :, at : at + LANES].astype(jnp.float32)

            window = [frame(index) for index in range(margin)]
            for t in range(block):
                window.append(frame(t + margin))
                terms = [weights[j] * window[j] for j in range(taps_count)]
                while len(terms) > 1:
                    terms = [terms[n] + terms[n + 1] for n in range(0, len(terms), 2)]
                rows[(part * channels + left) // LANES, pl.ds(t, inputs, stride=block), :] = terms[0]
                window = window[1:]
    tail[...] = volts_ref[:, :, (block - margin) * channels :]

    together = 2
    bins = table_ref.shape[0]

    def one(step, carry):
        first = pl.multiple_of(step * together * block, together * block)
        signal = jnp.concatenate(
            [rows[n, pl.ds(first, together * block), :].astype(jnp.bfloat16) for n in range(rows.shape[0])], axis=1
        )
        found = lax.dot_general(
            table_ref[...], signal, (((1,), (1,)), ((), ())), preferred_element_type=jnp.float32
        )
        for n in range(together):
            turned[pl.ds(step * together + n, bins, stride=inputs), :] = found[:, n * block : (n + 1) * block]
        return carry

    lax.fori_loop(0, inputs // together, one, 0)
    out_ref[...] = turned[...].astype(jnp.bfloat16).reshape(out_ref.shape)


def channelize(volts, history, taps, block):
    taps_count, channels = taps.shape
    _, inputs, samples = volts.shape
    spectra = samples // channels
    return pl.pallas_call(
        channelize_kernel,
        grid=(spectra // block,),
        in_specs=[
            pl.BlockSpec((2, inputs, block * channels), lambda n: (0, 0, n)),
            pl.BlockSpec(history.shape, lambda n: (0, 0, 0)),
            pl.BlockSpec(taps.shape, lambda n: (0, 0)),
            pl.BlockSpec((2 * channels, 2 * channels), lambda n: (0, 0)),
        ],
        out_specs=pl.BlockSpec((channels, 2, inputs, block), lambda n: (0, 0, 0, n)),
        out_shape=jax.ShapeDtypeStruct((channels, 2, inputs, spectra), jnp.bfloat16),
        scratch_shapes=[
            pltpu.VMEM(history.shape, jnp.bfloat16),
            pltpu.VMEM((2 * channels // LANES, inputs * block, LANES), jnp.float32),
            pltpu.VMEM((2 * channels * inputs, block), jnp.float32),
        ],
        compiler_params=pltpu.CompilerParams(vmem_limit_bytes=VMEM_BYTES),
        cost_estimate=pl.CostEstimate(
            flops=2 * spectra * inputs * (4 * channels * channels + 2 * taps_count * channels),
            bytes_accessed=16 * spectra * inputs * channels,
            transcendentals=0,
        ),
    )(volts, history, taps, jnp.asarray(dft_table(channels)))


def correlate_kernel(scale, tile, signal_ref, out_ref, store, sems):
    groups, bands, _, inputs, _ = signal_ref.shape
    total = bands * inputs
    width = tile // inputs

    def side(at, plane, sign=1):
        picked = [
            signal_ref[g, at * width : (at + 1) * width, plane].reshape(tile, -1) for g in range(groups)
        ]
        return [-x if sign < 0 else x for x in picked]

    def copy(n, p, q):
        place = out_ref.at[0, :, pl.ds(p * tile, tile), pl.ds(q * tile, tile)]
        return pltpu.make_async_copy(store.at[:, pl.ds(p * tile, tile), pl.ds(q * tile, tile)], place, sems.at[n])

    copies = []

    def put(p, q, real, imag):
        where = (pl.ds(p * tile, tile), pl.ds(q * tile, tile))
        store[0, where[0], where[1]] = real
        store[1, where[0], where[1]] = imag
        started = copy(len(copies), p, q)
        started.start()
        copies.append(started)

    contract = (((1,), (1,)), ((), ()))
    for p in range(total // tile):
        left = jnp.concatenate(side(p, 0) + side(p, 1), axis=1)
        crossed = jnp.concatenate(side(p, 1) + side(p, 0, -1), axis=1)
        for q in range(p + 1):
            right = jnp.concatenate(side(q, 0) + side(q, 1), axis=1)
            real = lax.dot_general(left, right, contract, preferred_element_type=jnp.float32) * scale
            imag = lax.dot_general(crossed, right, contract, preferred_element_type=jnp.float32) * scale
            put(p, q, real, imag)
            if p != q:
                put(q, p, real.T, -imag.T)
    for started in copies:
        started.wait()


def correlate(signal):
    groups, bands, _, inputs, spectra = signal.shape
    total = bands * inputs
    tile = 256
    blocks = (total // tile) ** 2
    return pl.pallas_call(
        functools.partial(correlate_kernel, 1.0 / (groups * spectra), tile),
        in_specs=[pl.BlockSpec(memory_space=pltpu.VMEM)],
        out_specs=pl.BlockSpec(memory_space=pl.ANY),
        out_shape=jax.ShapeDtypeStruct((1, 2, total, total), jnp.float32),
        scratch_shapes=[
            pltpu.VMEM((2, total, total), jnp.float32),
            pltpu.SemaphoreType.DMA((blocks,)),
        ],
        compiler_params=pltpu.CompilerParams(vmem_limit_bytes=VMEM_BYTES),
        cost_estimate=pl.CostEstimate(
            flops=5 * total * total * groups * spectra,
            bytes_accessed=8 * total * total,
            transcendentals=0,
        ),
    )(signal)


def per_device(volts, taps):
    time_groups = lax.axis_size("tm")
    band_groups = lax.axis_size("band")
    taps_count, channels = taps.shape
    _, inputs, samples = volts.shape
    margin = (taps_count - 1) * channels
    history = shifted(volts[:, :, samples - margin :], "tm", 1)
    spectra = channelize(volts, history, taps, LANES)
    turned = lax.all_to_all(spectra, ("tm", "band"), split_axis=0, concat_axis=0, tiled=True)
    return correlate(turned.reshape(time_groups, band_groups, 2, inputs, samples // channels))


def solution(mesh):
    in_specs = (P(None, "band", "tm"), P())
    out_specs = P(("tm", "band"), None, None, None)
    return jax.shard_map(
        per_device, mesh=mesh, in_specs=in_specs, out_specs=out_specs, check_vma=False
    )
```

```python
import functools
import math

import jax
import jax.numpy as jnp
import ml_dtypes
import numpy as np
from jax import lax
from jax.experimental import pallas as pl
from jax.experimental.pallas import tpu as pltpu
from jax.sharding import PartitionSpec as P

LANES = 128
SPARE = 8
VMEM_BYTES = 56 * 1024 * 1024


def dft_table(channels):
    index = np.arange(channels)
    theta = (index[:, None] * index[None, :] % channels) * (2.0 * math.pi / channels)
    factor = 1.0 / math.sqrt(channels)
    cosine = np.cos(theta) * factor
    sine = np.sin(theta) * factor
    real_row = np.stack([cosine, sine], axis=1)
    imag_row = np.stack([-sine, cosine], axis=1)
    table = np.stack([real_row, imag_row], axis=1)
    return table.reshape(2 * channels, 2 * channels).astype(np.float32).astype(ml_dtypes.bfloat16)


def filter_steps(volts, history, taps_ref, rows, pieces):
    taps_count, channels = taps_ref.shape
    inputs = volts.shape[1]
    block = volts.shape[2] // channels
    margin = taps_count - 1
    for part in range(2):
        for left in range(0, channels, LANES):
            weights = [taps_ref[j : j + 1, left : left + LANES] for j in range(taps_count)]

            def frame(index):
                if index < margin:
                    at = (index + 1) * channels + left
                    return history[part, :, at : at + LANES].astype(jnp.float32)
                at = (index - margin) * channels + left
                return volts[part, :, at : at + LANES].astype(jnp.float32)

            window = [frame(index) for index in range(margin)]
            for t in range(block):
                window.append(frame(t + margin))
                terms = [weights[j] * window[j] for j in range(taps_count)]
                while len(terms) > 1:
                    terms = [terms[n] + terms[n + 1] for n in range(0, len(terms), 2)]
                rows[(part * channels + left) // LANES, pl.ds(t, inputs, stride=block + SPARE), :] = terms[0]
                window = window[1:]
                if (t + 1) % (block // pieces) == 0:
                    yield


def dft_steps(table_ref, rows, turned, inputs, together):
    bins = table_ref.shape[0]
    block = LANES
    pitch = rows.shape[1] // inputs
    for step in range(inputs // together):
        signal = jnp.concatenate(
            [
                jnp.concatenate([rows[n, i * pitch : i * pitch + block, :].astype(jnp.bfloat16) for n in range(rows.shape[0])], axis=1)
                for i in range(step * together, (step + 1) * together)
            ],
            axis=0,
        )
        found = lax.dot_general(
            table_ref[...], signal, (((1,), (1,)), ((), ())), preferred_element_type=jnp.float32
        )
        for n in range(together):
            turned[pl.ds(step * together + n, bins, stride=inputs + SPARE), :] = found[:, n * block : (n + 1) * block]
        yield


def filter_kernel(volts_ref, history_ref, taps_ref, out_ref, rows):
    for _ in filter_steps(volts_ref, history_ref, taps_ref, rows, 1):
        pass
    inputs = volts_ref.shape[1]
    for i in range(inputs):
        first = i * (LANES + SPARE)
        out_ref[:, i * LANES : (i + 1) * LANES] = rows[:, first : first + LANES].astype(jnp.bfloat16)


def without_spare(turned, inputs):
    block = turned.shape[1]
    return turned[...].reshape(-1, inputs + SPARE, block)[:, :inputs].astype(jnp.bfloat16)


def channelize_kernel(
    filtered_ref, volts_ref, history_ref, taps_ref, table_ref, out_ref, rows, turned, late, early, sems
):
    inputs = volts_ref.shape[1]
    block = LANES
    steps = filter_steps(volts_ref, history_ref, taps_ref, rows, 2)
    for _ in dft_steps(table_ref, filtered_ref, turned, inputs, 2):
        next(steps)
    late[...] = without_spare(turned, inputs).reshape(late.shape)
    sent = [pltpu.make_async_copy(late, out_ref.at[:, :, :, pl.ds(block, block)], sems.at[0])]
    sent[0].start()
    for _ in dft_steps(table_ref, rows, turned, inputs, 2):
        pass
    early[...] = without_spare(turned, inputs).reshape(early.shape)
    sent.append(pltpu.make_async_copy(early, out_ref.at[:, :, :, pl.ds(0, block)], sems.at[1]))
    sent[1].start()
    for copy in sent:
        copy.wait()


def channelize(volts, history, taps):
    taps_count, channels = taps.shape
    _, inputs, samples = volts.shape
    spectra = samples // channels
    block = LANES
    reach = taps_count * channels
    halves = pl.BlockSpec((2, inputs, block * channels), lambda n: (0, 0, 1))
    tiles = 2 * channels // LANES
    rows = (tiles, inputs * block, LANES)
    spaced = (tiles, inputs * (block + SPARE), LANES)
    params = pltpu.CompilerParams(vmem_limit_bytes=VMEM_BYTES)
    filtered = pl.pallas_call(
        filter_kernel,
        grid=(1,),
        in_specs=[
            halves,
            pl.BlockSpec((2, inputs, reach), lambda n: (0, 0, block // taps_count - 1)),
            pl.BlockSpec(taps.shape, lambda n: (0, 0)),
        ],
        out_specs=pl.BlockSpec(rows, lambda n: (0, 0, 0)),
        out_shape=jax.ShapeDtypeStruct(rows, jnp.bfloat16),
        scratch_shapes=[pltpu.VMEM(spaced, jnp.float32)],
        compiler_params=params,
        cost_estimate=pl.CostEstimate(
            flops=4 * taps_count * block * inputs * channels,
            bytes_accessed=8 * block * inputs * channels,
            transcendentals=0,
        ),
    )(volts, volts, taps)
    return pl.pallas_call(
        channelize_kernel,
        grid=(1,),
        in_specs=[
            pl.BlockSpec(rows, lambda n: (0, 0, 0)),
            pl.BlockSpec((2, inputs, block * channels), lambda n: (0, 0, 0)),
            pl.BlockSpec(history.shape, lambda n: (0, 0, 0)),
            pl.BlockSpec(taps.shape, lambda n: (0, 0)),
            pl.BlockSpec((2 * channels, 2 * channels), lambda n: (0, 0)),
        ],
        out_specs=pl.BlockSpec(memory_space=pl.ANY),
        out_shape=jax.ShapeDtypeStruct((channels, 2, inputs, spectra), jnp.bfloat16),
        scratch_shapes=[
            pltpu.VMEM(spaced, jnp.float32),
            pltpu.VMEM((2 * channels * (inputs + SPARE), block), jnp.float32),
            pltpu.VMEM((channels, 2, inputs, block), jnp.bfloat16),
            pltpu.VMEM((channels, 2, inputs, block), jnp.bfloat16),
            pltpu.SemaphoreType.DMA((2,)),
        ],
        compiler_params=params,
        cost_estimate=pl.CostEstimate(
            flops=8 * spectra * inputs * channels * channels,
            bytes_accessed=12 * spectra * inputs * channels,
            transcendentals=0,
        ),
    )(filtered, volts, history, taps, jnp.asarray(dft_table(channels)))


def correlate_kernel(scale, tile, signal_ref, out_ref, here, plain, crossed, store, in_sems, out_sems):
    groups, bands, _, inputs, times = signal_ref.shape
    total = bands * inputs
    half_depth = groups * times
    arriving = [pltpu.make_async_copy(signal_ref.at[g], here.at[g], in_sems.at[g]) for g in range(groups)]
    for copy in arriving:
        copy.start()
    for g in range(groups):
        arriving[g].wait()
        real = here[g, :, 0].reshape(total, times)
        imag = here[g, :, 1].reshape(total, times)
        low, high = g * times, half_depth + g * times
        plain[:, low : low + times] = real
        plain[:, high : high + times] = imag
        crossed[:, low : low + times] = imag
        crossed[:, high : high + times] = -real

    contract = (((1,), (1,)), ((), ()))
    copies = []

    def send(p, rows, q, columns):
        where = (slice(None), pl.ds(p, rows), pl.ds(q, columns))
        copy = pltpu.make_async_copy(store.at[where], out_ref.at[(0, *where)], out_sems.at[len(copies)])
        copy.start()
        copies.append(copy)

    for q in range(0, total, tile):
        right = plain[q : q + tile, :]
        real = lax.dot_general(plain[q:, :], right, contract, preferred_element_type=jnp.float32) * scale
        imag = lax.dot_general(crossed[q:, :], right, contract, preferred_element_type=jnp.float32) * scale
        store[0, q:, q : q + tile] = real
        store[1, q:, q : q + tile] = imag
        send(q, total - q, q, tile)
        if q + tile < total:
            store[0, q : q + tile, q + tile :] = real[tile:].T
            store[1, q : q + tile, q + tile :] = -(imag[tile:].T)
            send(q, tile, q + tile, total - q - tile)
    for copy in copies:
        copy.wait()


def correlate(signal):
    groups, bands, _, inputs, times = signal.shape
    total = bands * inputs
    spectra = groups * times
    tile = 256
    return pl.pallas_call(
        functools.partial(correlate_kernel, 1.0 / spectra, tile),
        in_specs=[pl.BlockSpec(memory_space=pl.ANY)],
        out_specs=pl.BlockSpec(memory_space=pl.ANY),
        out_shape=jax.ShapeDtypeStruct((1, 2, total, total), jnp.float32),
        scratch_shapes=[
            pltpu.VMEM(signal.shape, jnp.bfloat16),
            pltpu.VMEM((total, 2 * spectra), jnp.bfloat16),
            pltpu.VMEM((total, 2 * spectra), jnp.bfloat16),
            pltpu.VMEM((2, total, total), jnp.float32),
            pltpu.SemaphoreType.DMA((groups,)),
            pltpu.SemaphoreType.DMA((2 * (total // tile) - 1,)),
        ],
        compiler_params=pltpu.CompilerParams(vmem_limit_bytes=VMEM_BYTES),
        cost_estimate=pl.CostEstimate(
            flops=5 * total * total * spectra, bytes_accessed=12 * total * total, transcendentals=0
        ),
    )(signal)


def per_device(volts, taps):
    time_groups = lax.axis_size("tm")
    band_groups = lax.axis_size("band")
    taps_count, channels = taps.shape
    _, inputs, samples = volts.shape
    reach = taps_count * channels
    history = lax.ppermute(volts[:, :, samples - reach :], "tm", [(i, i + 1) for i in range(time_groups - 1)])
    spectra = channelize(volts, history, taps)
    turned = lax.all_to_all(spectra, ("tm", "band"), split_axis=0, concat_axis=0, tiled=True)
    return correlate(turned.reshape(time_groups, band_groups, 2, inputs, samples // channels))


def solution(mesh):
    in_specs = (P(None, "band", "tm"), P())
    out_specs = P(("tm", "band"), None, None, None)
    return jax.shard_map(
        per_device, mesh=mesh, in_specs=in_specs, out_specs=out_specs, check_vma=False
    )
```

```python
import functools
import math

import jax
import jax.numpy as jnp
import ml_dtypes
import numpy as np
from jax import lax
from jax.experimental import pallas as pl
from jax.experimental.pallas import tpu as pltpu
from jax.sharding import PartitionSpec as P

LANES = 128
SPARE = 8
VMEM_BYTES = 56 * 1024 * 1024


def dft_table(channels):
    index = np.arange(channels)
    theta = (index[:, None] * index[None, :] % channels) * (2.0 * math.pi / channels)
    factor = 1.0 / math.sqrt(channels)
    cosine = np.cos(theta) * factor
    sine = np.sin(theta) * factor
    real_row = np.stack([cosine, sine], axis=1)
    imag_row = np.stack([-sine, cosine], axis=1)
    table = np.stack([real_row, imag_row], axis=1)
    return table.reshape(2 * channels, 2 * channels).astype(np.float32).astype(ml_dtypes.bfloat16)


def filter_steps(volts, history, taps_ref, rows, pieces):
    taps_count, channels = taps_ref.shape
    inputs = volts.shape[1]
    block = volts.shape[2] // channels
    margin = taps_count - 1
    for part in range(2):
        for left in range(0, channels, LANES):
            weights = [taps_ref[j : j + 1, left : left + LANES] for j in range(taps_count)]

            def frame(index):
                if index < margin:
                    at = (index + 1) * channels + left
                    return history[part, :, at : at + LANES].astype(jnp.float32)
                at = (index - margin) * channels + left
                return volts[part, :, at : at + LANES].astype(jnp.float32)

            window = [frame(index) for index in range(margin)]
            for t in range(block):
                window.append(frame(t + margin))
                terms = [weights[j] * window[j] for j in range(taps_count)]
                while len(terms) > 1:
                    terms = [terms[n] + terms[n + 1] for n in range(0, len(terms), 2)]
                rows[(part * channels + left) // LANES, pl.ds(t, inputs, stride=block + SPARE), :] = terms[0]
                window = window[1:]
                if (t + 1) % (block // pieces) == 0:
                    yield


def dft_steps(table_ref, rows, turned, inputs, together):
    bins = table_ref.shape[0]
    block = LANES
    pitch = rows.shape[1] // inputs
    for step in range(inputs // together):
        signal = jnp.concatenate(
            [
                jnp.concatenate([rows[n, i * pitch : i * pitch + block, :].astype(jnp.bfloat16) for n in range(rows.shape[0])], axis=1)
                for i in range(step * together, (step + 1) * together)
            ],
            axis=0,
        )
        found = lax.dot_general(
            table_ref[...], signal, (((1,), (1,)), ((), ())), preferred_element_type=jnp.float32
        )
        for n in range(together):
            turned[pl.ds(step * together + n, bins, stride=inputs + SPARE), :] = found[:, n * block : (n + 1) * block]
        yield


def rounding_steps(turned, out, inputs, pieces):
    channels, _, _, block = out.shape
    part = channels // pieces
    pitch = inputs + SPARE
    for n in range(pieces):
        found = turned[2 * n * part * pitch : 2 * (n + 1) * part * pitch, :].reshape(2 * part, pitch, block)
        out[n * part : (n + 1) * part] = found[:, :inputs].astype(jnp.bfloat16).reshape(part, 2, inputs, block)
        yield pl.ds(n * part, part)


def channelize_kernel(
    volts_ref, history_ref, taps_ref, table_ref, out_ref, volts, before, rows, turned, rounded, in_sems, out_sems
):
    inputs = volts_ref.shape[1]
    taps_count, channels = taps_ref.shape
    block = LANES
    width = block * channels
    reach = taps_count * channels
    ahead = pltpu.make_async_copy(volts_ref.at[:, :, pl.ds(width - reach, reach)], before, in_sems.at[2, 0])
    ahead.start()
    arriving = {}
    for half in (1, 0):
        for part in range(2):
            copy = pltpu.make_async_copy(
                volts_ref.at[part, :, pl.ds(half * width, width)], volts.at[half, part], in_sems.at[half, part]
            )
            copy.start()
            arriving[half, part] = copy

    pieces = 4
    ahead.wait()
    arriving[1, 0].wait()
    late = filter_steps(volts.at[1], before, taps_ref, rows.at[1], pieces)
    for n in range(2 * channels // LANES * pieces):
        if n == channels // LANES * pieces:
            arriving[1, 1].wait()
        next(late)
    arriving[0, 0].wait()
    arriving[0, 1].wait()
    early = filter_steps(volts.at[0], history_ref, taps_ref, rows.at[0], pieces)
    for _ in dft_steps(table_ref, rows.at[1], turned.at[1], inputs, 2):
        next(early)
        next(early)
    sent = []

    def send(half, where):
        copy = pltpu.make_async_copy(
            rounded.at[half, where], out_ref.at[where, :, :, pl.ds(half * block, block)], out_sems.at[len(sent)]
        )
        copy.start()
        sent.append(copy)

    steps = dft_steps(table_ref, rows.at[0], turned.at[0], inputs, 2)
    for where in rounding_steps(turned.at[1], rounded.at[1], inputs, inputs // 2):
        send(1, where)
        next(steps)
    for where in rounding_steps(turned.at[0], rounded.at[0], inputs, 4):
        send(0, where)
    for copy in sent:
        copy.wait()


def channelize(volts, history, taps):
    taps_count, channels = taps.shape
    _, inputs, samples = volts.shape
    spectra = samples // channels
    block = LANES
    resident = pl.BlockSpec(memory_space=pltpu.VMEM)
    return pl.pallas_call(
        channelize_kernel,
        in_specs=[pl.BlockSpec(memory_space=pl.ANY), resident, resident, resident],
        out_specs=pl.BlockSpec(memory_space=pl.ANY),
        out_shape=jax.ShapeDtypeStruct((channels, 2, inputs, spectra), jnp.bfloat16),
        scratch_shapes=[
            pltpu.VMEM((2, 2, inputs, block * channels), jnp.bfloat16),
            pltpu.VMEM((2, inputs, taps_count * channels), jnp.bfloat16),
            pltpu.VMEM((2, 2 * channels // LANES, inputs * (block + SPARE), LANES), jnp.float32),
            pltpu.VMEM((2, 2 * channels * (inputs + SPARE), block), jnp.float32),
            pltpu.VMEM((2, channels, 2, inputs, block), jnp.bfloat16),
            pltpu.SemaphoreType.DMA((3, 2)),
            pltpu.SemaphoreType.DMA((inputs // 2 + 4,)),
        ],
        compiler_params=pltpu.CompilerParams(vmem_limit_bytes=VMEM_BYTES),
        cost_estimate=pl.CostEstimate(
            flops=8 * spectra * inputs * channels * channels,
            bytes_accessed=8 * spectra * inputs * channels,
            transcendentals=0,
        ),
    )(volts, history, taps, jnp.asarray(dft_table(channels)))


def correlate_kernel(scale, tile, signal_ref, out_ref, here, plain, crossed, store, in_sems, out_sems):
    groups, bands, _, inputs, times = signal_ref.shape
    total = bands * inputs
    half_depth = groups * times
    width = tile // inputs
    arriving = []
    for n in range(total // tile):
        where = (slice(None), pl.ds(n * width, width))
        arriving.append(pltpu.make_async_copy(signal_ref.at[where], here.at[where], in_sems.at[n]))
        arriving[n].start()

    contract = (((1,), (1,)), ((), ()))
    copies = []

    def put(p, q, real, imag):
        where = (slice(None), pl.ds(p, tile), pl.ds(q, tile))
        store[0, p : p + tile, q : q + tile] = real
        store[1, p : p + tile, q : q + tile] = imag
        copy = pltpu.make_async_copy(store.at[where], out_ref.at[(0, *where)], out_sems.at[len(copies)])
        copy.start()
        copies.append(copy)

    for n in range(total // tile):
        arriving[n].wait()
        p = n * tile
        for g in range(groups):
            real = here[g, n * width : (n + 1) * width, 0].reshape(tile, times)
            imag = here[g, n * width : (n + 1) * width, 1].reshape(tile, times)
            low, high = g * times, half_depth + g * times
            plain[p : p + tile, low : low + times] = real
            plain[p : p + tile, high : high + times] = imag
            crossed[p : p + tile, low : low + times] = imag
            crossed[p : p + tile, high : high + times] = -real
        for q in range(0, p + tile, tile):
            right = plain[q : q + tile, :]
            real = lax.dot_general(plain[p : p + tile, :], right, contract, preferred_element_type=jnp.float32) * scale
            imag = lax.dot_general(crossed[p : p + tile, :], right, contract, preferred_element_type=jnp.float32) * scale
            put(p, q, real, imag)
            if p != q:
                put(q, p, real.T, -imag.T)
    for copy in copies:
        copy.wait()


def correlate(signal):
    groups, bands, _, inputs, times = signal.shape
    total = bands * inputs
    spectra = groups * times
    tile = 256
    return pl.pallas_call(
        functools.partial(correlate_kernel, 1.0 / spectra, tile),
        in_specs=[pl.BlockSpec(memory_space=pl.ANY)],
        out_specs=pl.BlockSpec(memory_space=pl.ANY),
        out_shape=jax.ShapeDtypeStruct((1, 2, total, total), jnp.float32),
        scratch_shapes=[
            pltpu.VMEM(signal.shape, jnp.bfloat16),
            pltpu.VMEM((total, 2 * spectra), jnp.bfloat16),
            pltpu.VMEM((total, 2 * spectra), jnp.bfloat16),
            pltpu.VMEM((2, total, total), jnp.float32),
            pltpu.SemaphoreType.DMA((total // tile,)),
            pltpu.SemaphoreType.DMA(((total // tile) ** 2,)),
        ],
        compiler_params=pltpu.CompilerParams(vmem_limit_bytes=VMEM_BYTES),
        cost_estimate=pl.CostEstimate(
            flops=5 * total * total * spectra, bytes_accessed=12 * total * total, transcendentals=0
        ),
    )(signal)


def per_device(volts, taps):
    time_groups = lax.axis_size("tm")
    band_groups = lax.axis_size("band")
    taps_count, channels = taps.shape
    _, inputs, samples = volts.shape
    reach = taps_count * channels
    history = lax.ppermute(volts[:, :, samples - reach :], "tm", [(i, i + 1) for i in range(time_groups - 1)])
    spectra = channelize(volts, history, taps)
    turned = lax.all_to_all(spectra, ("tm", "band"), split_axis=0, concat_axis=0, tiled=True)
    return correlate(turned.reshape(time_groups, band_groups, 2, inputs, samples // channels))


def solution(mesh):
    in_specs = (P(None, "band", "tm"), P())
    out_specs = P(("tm", "band"), None, None, None)
    return jax.shard_map(
        per_device, mesh=mesh, in_specs=in_specs, out_specs=out_specs, check_vma=False
    )
```

```python
import functools
import math

import jax
import jax.numpy as jnp
import ml_dtypes
import numpy as np
from jax import lax
from jax.experimental import pallas as pl
from jax.experimental.pallas import tpu as pltpu
from jax.sharding import PartitionSpec as P

LANES = 128
SPARE = 8
VMEM_BYTES = 56 * 1024 * 1024
LATE_VMEM_BYTES = 24 * 1024 * 1024


def dft_table(channels):
    index = np.arange(channels)
    theta = (index[:, None] * index[None, :] % channels) * (2.0 * math.pi / channels)
    factor = 1.0 / math.sqrt(channels)
    cosine = np.cos(theta) * factor
    sine = np.sin(theta) * factor
    real_row = np.stack([cosine, sine], axis=1)
    imag_row = np.stack([-sine, cosine], axis=1)
    table = np.stack([real_row, imag_row], axis=1)
    return table.reshape(2 * channels, 2 * channels).astype(np.float32).astype(ml_dtypes.bfloat16)


def filter_steps(volts, history, taps_ref, rows, pieces):
    taps_count, channels = taps_ref.shape
    inputs = volts.shape[1]
    block = volts.shape[2] // channels
    margin = taps_count - 1
    for part in range(2):
        for left in range(0, channels, LANES):
            weights = [taps_ref[j : j + 1, left : left + LANES] for j in range(taps_count)]

            def frame(index):
                if index < margin:
                    at = (index + 1) * channels + left
                    return history[part, :, at : at + LANES].astype(jnp.float32)
                at = (index - margin) * channels + left
                return volts[part, :, at : at + LANES].astype(jnp.float32)

            window = [frame(index) for index in range(margin)]
            for t in range(block):
                window.append(frame(t + margin))
                terms = [weights[j] * window[j] for j in range(taps_count)]
                while len(terms) > 1:
                    terms = [terms[n] + terms[n + 1] for n in range(0, len(terms), 2)]
                rows[(part * channels + left) // LANES, pl.ds(t, inputs, stride=block + SPARE), :] = terms[0]
                window = window[1:]
                if (t + 1) % (block // pieces) == 0:
                    yield


def dft_steps(table_ref, rows, turned, inputs, together):
    bins = table_ref.shape[0]
    block = LANES
    pitch = rows.shape[1] // inputs
    for step in range(inputs // together):
        signal = jnp.concatenate(
            [
                jnp.concatenate([rows[n, i * pitch : i * pitch + block, :].astype(jnp.bfloat16) for n in range(rows.shape[0])], axis=1)
                for i in range(step * together, (step + 1) * together)
            ],
            axis=0,
        )
        found = lax.dot_general(
            table_ref[...], signal, (((1,), (1,)), ((), ())), preferred_element_type=jnp.float32
        )
        for n in range(together):
            turned[pl.ds(step * together + n, bins, stride=inputs + SPARE), :] = found[:, n * block : (n + 1) * block]
        yield


def rounding_steps(turned, out, inputs, pieces):
    channels, _, _, block = out.shape
    part = channels // pieces
    pitch = inputs + SPARE
    for n in range(pieces):
        found = turned[2 * n * part * pitch : 2 * (n + 1) * part * pitch, :].reshape(2 * part, pitch, block)
        out[n * part : (n + 1) * part] = found[:, :inputs].astype(jnp.bfloat16).reshape(part, 2, inputs, block)
        yield pl.ds(n * part, part)


def channelize_kernel(
    volts_ref, history_ref, taps_ref, table_ref, out_ref, volts, before, rows, turned, rounded, in_sems, out_sems
):
    inputs = volts_ref.shape[1]
    taps_count, channels = taps_ref.shape
    block = LANES
    width = block * channels
    reach = taps_count * channels
    ahead = pltpu.make_async_copy(volts_ref.at[:, :, pl.ds(width - reach, reach)], before, in_sems.at[2, 0])
    ahead.start()
    arriving = {}
    for half in (1, 0):
        for part in range(2):
            copy = pltpu.make_async_copy(
                volts_ref.at[part, :, pl.ds(half * width, width)], volts.at[half, part], in_sems.at[half, part]
            )
            copy.start()
            arriving[half, part] = copy

    pieces = 4
    ahead.wait()
    arriving[1, 0].wait()
    late = filter_steps(volts.at[1], before, taps_ref, rows.at[1], pieces)
    for n in range(2 * channels // LANES * pieces):
        if n == channels // LANES * pieces:
            arriving[1, 1].wait()
        next(late)
    arriving[0, 0].wait()
    arriving[0, 1].wait()
    early = filter_steps(volts.at[0], history_ref, taps_ref, rows.at[0], pieces)
    for _ in dft_steps(table_ref, rows.at[1], turned.at[1], inputs, 2):
        next(early)
        next(early)
    sent = []

    def send(half, where):
        copy = pltpu.make_async_copy(
            rounded.at[half, where], out_ref.at[where, :, :, pl.ds(half * block, block)], out_sems.at[len(sent)]
        )
        copy.start()
        sent.append(copy)

    steps = dft_steps(table_ref, rows.at[0], turned.at[0], inputs, 2)
    for where in rounding_steps(turned.at[1], rounded.at[1], inputs, inputs // 2):
        send(1, where)
        next(steps)
    for where in rounding_steps(turned.at[0], rounded.at[0], inputs, 4):
        send(0, where)
    for copy in sent:
        copy.wait()


def channelize(volts, history, taps):
    taps_count, channels = taps.shape
    _, inputs, samples = volts.shape
    spectra = samples // channels
    block = LANES
    resident = pl.BlockSpec(memory_space=pltpu.VMEM)
    return pl.pallas_call(
        channelize_kernel,
        in_specs=[pl.BlockSpec(memory_space=pl.ANY), resident, resident, resident],
        out_specs=pl.BlockSpec(memory_space=pl.ANY),
        out_shape=jax.ShapeDtypeStruct((channels, 2, inputs, spectra), jnp.bfloat16),
        scratch_shapes=[
            pltpu.VMEM((2, 2, inputs, block * channels), jnp.bfloat16),
            pltpu.VMEM((2, inputs, taps_count * channels), jnp.bfloat16),
            pltpu.VMEM((2, 2 * channels // LANES, inputs * (block + SPARE), LANES), jnp.float32),
            pltpu.VMEM((2, 2 * channels * (inputs + SPARE), block), jnp.float32),
            pltpu.VMEM((2, channels, 2, inputs, block), jnp.bfloat16),
            pltpu.SemaphoreType.DMA((3, 2)),
            pltpu.SemaphoreType.DMA((inputs // 2 + 4,)),
        ],
        compiler_params=pltpu.CompilerParams(vmem_limit_bytes=VMEM_BYTES),
        cost_estimate=pl.CostEstimate(
            flops=8 * spectra * inputs * channels * channels,
            bytes_accessed=8 * spectra * inputs * channels,
            transcendentals=0,
        ),
    )(volts, history, taps, jnp.asarray(dft_table(channels)))


def correlate_kernel(scale, tile, here, out_ref, plain, crossed, store, out_sems):
    groups, bands, _, inputs, times = here.shape
    total = bands * inputs
    half_depth = groups * times
    width = tile // inputs
    contract = (((1,), (1,)), ((), ()))
    copies = []

    def put(p, q, real, imag):
        where = (slice(None), pl.ds(p, tile), pl.ds(q, tile))
        store[0, p : p + tile, q : q + tile] = real
        store[1, p : p + tile, q : q + tile] = imag
        copy = pltpu.make_async_copy(store.at[where], out_ref.at[(0, *where)], out_sems.at[len(copies)])
        copy.start()
        copies.append(copy)

    for n in range(total // tile):
        p = n * tile
        for g in range(groups):
            real = here[g, n * width : (n + 1) * width, 0].reshape(tile, times)
            imag = here[g, n * width : (n + 1) * width, 1].reshape(tile, times)
            low, high = g * times, half_depth + g * times
            plain[p : p + tile, low : low + times] = real
            plain[p : p + tile, high : high + times] = imag
            crossed[p : p + tile, low : low + times] = imag
            crossed[p : p + tile, high : high + times] = -real
        for q in range(0, p + tile, tile):
            right = plain[q : q + tile, :]
            real = lax.dot_general(plain[p : p + tile, :], right, contract, preferred_element_type=jnp.float32) * scale
            imag = lax.dot_general(crossed[p : p + tile, :], right, contract, preferred_element_type=jnp.float32) * scale
            put(p, q, real, imag)
            if p != q:
                put(q, p, real.T, -imag.T)
    for copy in copies:
        copy.wait()


def correlate(signal):
    groups, bands, _, inputs, times = signal.shape
    total = bands * inputs
    spectra = groups * times
    tile = 256
    return pl.pallas_call(
        functools.partial(correlate_kernel, 1.0 / spectra, tile),
        in_specs=[pl.BlockSpec(memory_space=pltpu.VMEM)],
        out_specs=pl.BlockSpec(memory_space=pl.ANY),
        out_shape=jax.ShapeDtypeStruct((1, 2, total, total), jnp.float32),
        scratch_shapes=[
            pltpu.VMEM((total, 2 * spectra), jnp.bfloat16),
            pltpu.VMEM((total, 2 * spectra), jnp.bfloat16),
            pltpu.VMEM((2, total, total), jnp.float32),
            pltpu.SemaphoreType.DMA(((total // tile) ** 2,)),
        ],
        compiler_params=pltpu.CompilerParams(vmem_limit_bytes=LATE_VMEM_BYTES),
        cost_estimate=pl.CostEstimate(
            flops=5 * total * total * spectra, bytes_accessed=12 * total * total, transcendentals=0
        ),
    )(signal)


def per_device(volts, taps):
    time_groups = lax.axis_size("tm")
    band_groups = lax.axis_size("band")
    taps_count, channels = taps.shape
    _, inputs, samples = volts.shape
    reach = taps_count * channels
    history = lax.ppermute(volts[:, :, samples - reach :], "tm", [(i, i + 1) for i in range(time_groups - 1)])
    spectra = channelize(volts, history, taps)
    turned = lax.all_to_all(spectra, ("tm", "band"), split_axis=0, concat_axis=0, tiled=True)
    return correlate(turned.reshape(time_groups, band_groups, 2, inputs, samples // channels))


def solution(mesh):
    in_specs = (P(None, "band", "tm"), P())
    out_specs = P(("tm", "band"), None, None, None)
    return jax.shard_map(
        per_device, mesh=mesh, in_specs=in_specs, out_specs=out_specs, check_vma=False
    )
```

```python
import functools
import math

import jax
import jax.numpy as jnp
import ml_dtypes
import numpy as np
from jax import lax
from jax.experimental import pallas as pl
from jax.experimental.pallas import tpu as pltpu
from jax.sharding import PartitionSpec as P

LANES = 128
SPARE = 8
VMEM_BYTES = 56 * 1024 * 1024
LATE_VMEM_BYTES = 24 * 1024 * 1024


def dft_table(channels):
    index = np.arange(channels)
    theta = (index[:, None] * index[None, :] % channels) * (2.0 * math.pi / channels)
    factor = 1.0 / math.sqrt(channels)
    cosine = np.cos(theta) * factor
    sine = np.sin(theta) * factor
    real_row = np.stack([cosine, sine], axis=1)
    imag_row = np.stack([-sine, cosine], axis=1)
    table = np.stack([real_row, imag_row], axis=1)
    return table.reshape(2 * channels, 2 * channels).astype(np.float32).astype(ml_dtypes.bfloat16)


def filter_steps(volts, history, taps_ref, rows, pieces):
    taps_count, channels = taps_ref.shape
    inputs = volts.shape[1]
    block = volts.shape[2] // channels
    margin = taps_count - 1
    for part in range(2):
        for left in range(0, channels, LANES):
            weights = [taps_ref[j : j + 1, left : left + LANES] for j in range(taps_count)]

            def frame(index):
                if index < margin:
                    at = (index + 1) * channels + left
                    return history[part, :, at : at + LANES].astype(jnp.float32)
                at = (index - margin) * channels + left
                return volts[part, :, at : at + LANES].astype(jnp.float32)

            window = [frame(index) for index in range(margin)]
            for t in range(block):
                window.append(frame(t + margin))
                terms = [weights[j] * window[j] for j in range(taps_count)]
                while len(terms) > 1:
                    terms = [terms[n] + terms[n + 1] for n in range(0, len(terms), 2)]
                rows[(part * channels + left) // LANES, pl.ds(t, inputs, stride=block + SPARE), :] = terms[0]
                window = window[1:]
                if (t + 1) % (block // pieces) == 0:
                    yield


def dft_steps(table_ref, rows, turned, inputs, together):
    bins = table_ref.shape[0]
    block = LANES
    pitch = rows.shape[1] // inputs
    for step in range(inputs // together):
        signal = jnp.concatenate(
            [
                jnp.concatenate([rows[n, i * pitch : i * pitch + block, :].astype(jnp.bfloat16) for n in range(rows.shape[0])], axis=1)
                for i in range(step * together, (step + 1) * together)
            ],
            axis=0,
        )
        found = lax.dot_general(
            table_ref[...], signal, (((1,), (1,)), ((), ())), preferred_element_type=jnp.float32
        )
        for n in range(together):
            turned[pl.ds(step * together + n, bins, stride=inputs + SPARE), :] = found[:, n * block : (n + 1) * block]
        yield


def rounding_steps(turned, out, inputs, pieces):
    channels, _, _, block = out.shape
    part = channels // pieces
    pitch = inputs + SPARE
    for n in range(pieces):
        found = turned[2 * n * part * pitch : 2 * (n + 1) * part * pitch, :].reshape(2 * part, pitch, block)
        out[n * part : (n + 1) * part] = found[:, :inputs].astype(jnp.bfloat16).reshape(part, 2, inputs, block)
        yield pl.ds(n * part, part)


def channelize_kernel(
    volts_ref, history_ref, taps_ref, table_ref, out_ref, volts, table, before, rows, turned, rounded, in_sems, out_sems
):
    inputs = volts_ref.shape[1]
    taps_count, channels = taps_ref.shape
    block = LANES
    width = block * channels
    reach = taps_count * channels
    pieces = 4
    ahead = pltpu.make_async_copy(volts_ref.at[:, :, pl.ds(width - reach, reach)], before, in_sems.at[2, 0, 0])
    ahead.start()
    arriving = {}
    for half in (1, 0):
        for part in range(2):
            for n in range(pieces):
                copy = pltpu.make_async_copy(
                    volts_ref.at[part, :, pl.ds(half * width + n * (width // pieces), width // pieces)],
                    volts.at[half, part, :, pl.ds(n * (width // pieces), width // pieces)],
                    in_sems.at[half, part, n],
                )
                copy.start()
                arriving[half, part, n] = copy
        if half == 1:
            tables = pltpu.make_async_copy(table_ref, table, in_sems.at[2, 1, 0])
            tables.start()

    ahead.wait()
    late = filter_steps(volts.at[1], before, taps_ref, rows.at[1], pieces)
    for n in range(2 * channels // LANES * pieces):
        part, tile_piece = divmod(n, channels // LANES * pieces)
        if tile_piece < pieces:
            arriving[1, part, tile_piece].wait()
        next(late)
    for part in range(2):
        for n in range(pieces):
            arriving[0, part, n].wait()
    tables.wait()
    early = filter_steps(volts.at[0], history_ref, taps_ref, rows.at[0], pieces)
    for _ in dft_steps(table, rows.at[1], turned.at[1], inputs, 2):
        next(early)
        next(early)
    sent = []

    def send(half, where):
        copy = pltpu.make_async_copy(
            rounded.at[half, where], out_ref.at[where, :, :, pl.ds(half * block, block)], out_sems.at[len(sent)]
        )
        copy.start()
        sent.append(copy)

    steps = dft_steps(table, rows.at[0], turned.at[0], inputs, 2)
    for where in rounding_steps(turned.at[1], rounded.at[1], inputs, inputs // 2):
        send(1, where)
        next(steps)
    for where in rounding_steps(turned.at[0], rounded.at[0], inputs, 4):
        send(0, where)
    for copy in sent:
        copy.wait()


def channelize(volts, history, taps):
    taps_count, channels = taps.shape
    _, inputs, samples = volts.shape
    spectra = samples // channels
    block = LANES
    resident = pl.BlockSpec(memory_space=pltpu.VMEM)
    return pl.pallas_call(
        channelize_kernel,
        in_specs=[pl.BlockSpec(memory_space=pl.ANY), resident, resident, pl.BlockSpec(memory_space=pl.ANY)],
        out_specs=pl.BlockSpec(memory_space=pl.ANY),
        out_shape=jax.ShapeDtypeStruct((channels, 2, inputs, spectra), jnp.bfloat16),
        scratch_shapes=[
            pltpu.VMEM((2, 2, inputs, block * channels), jnp.bfloat16),
            pltpu.VMEM((2 * channels, 2 * channels), jnp.bfloat16),
            pltpu.VMEM((2, inputs, taps_count * channels), jnp.bfloat16),
            pltpu.VMEM((2, 2 * channels // LANES, inputs * (block + SPARE), LANES), jnp.float32),
            pltpu.VMEM((2, 2 * channels * (inputs + SPARE), block), jnp.float32),
            pltpu.VMEM((2, channels, 2, inputs, block), jnp.bfloat16),
            pltpu.SemaphoreType.DMA((3, 2, 4)),
            pltpu.SemaphoreType.DMA((inputs // 2 + 4,)),
        ],
        compiler_params=pltpu.CompilerParams(vmem_limit_bytes=VMEM_BYTES),
        cost_estimate=pl.CostEstimate(
            flops=8 * spectra * inputs * channels * channels,
            bytes_accessed=8 * spectra * inputs * channels,
            transcendentals=0,
        ),
    )(volts, history, taps, jnp.asarray(dft_table(channels)))


def correlate_kernel(scale, tile, here, out_ref, plain, crossed, store, out_sems):
    groups, bands, _, inputs, times = here.shape
    total = bands * inputs
    half_depth = groups * times
    width = tile // inputs
    contract = (((1,), (1,)), ((), ()))
    copies = []

    def put(p, q, real, imag):
        where = (slice(None), pl.ds(p, tile), pl.ds(q, tile))
        store[0, p : p + tile, q : q + tile] = real
        store[1, p : p + tile, q : q + tile] = imag
        copy = pltpu.make_async_copy(store.at[where], out_ref.at[(0, *where)], out_sems.at[len(copies)])
        copy.start()
        copies.append(copy)

    for n in range(total // tile):
        p = n * tile
        for g in range(groups):
            real = here[g, n * width : (n + 1) * width, 0].reshape(tile, times)
            imag = here[g, n * width : (n + 1) * width, 1].reshape(tile, times)
            low, high = g * times, half_depth + g * times
            plain[p : p + tile, low : low + times] = real
            plain[p : p + tile, high : high + times] = imag
            crossed[p : p + tile, low : low + times] = imag
            crossed[p : p + tile, high : high + times] = -real
        for q in range(0, p + tile, tile):
            right = plain[q : q + tile, :]
            real = lax.dot_general(plain[p : p + tile, :], right, contract, preferred_element_type=jnp.float32) * scale
            imag = lax.dot_general(crossed[p : p + tile, :], right, contract, preferred_element_type=jnp.float32) * scale
            put(p, q, real, imag)
            if p != q:
                put(q, p, real.T, -imag.T)
    for copy in copies:
        copy.wait()


def correlate(signal):
    groups, bands, _, inputs, times = signal.shape
    total = bands * inputs
    spectra = groups * times
    tile = 256
    return pl.pallas_call(
        functools.partial(correlate_kernel, 1.0 / spectra, tile),
        in_specs=[pl.BlockSpec(memory_space=pltpu.VMEM)],
        out_specs=pl.BlockSpec(memory_space=pl.ANY),
        out_shape=jax.ShapeDtypeStruct((1, 2, total, total), jnp.float32),
        scratch_shapes=[
            pltpu.VMEM((total, 2 * spectra), jnp.bfloat16),
            pltpu.VMEM((total, 2 * spectra), jnp.bfloat16),
            pltpu.VMEM((2, total, total), jnp.float32),
            pltpu.SemaphoreType.DMA(((total // tile) ** 2,)),
        ],
        compiler_params=pltpu.CompilerParams(vmem_limit_bytes=LATE_VMEM_BYTES),
        cost_estimate=pl.CostEstimate(
            flops=5 * total * total * spectra, bytes_accessed=12 * total * total, transcendentals=0
        ),
    )(signal)


def per_device(volts, taps):
    time_groups = lax.axis_size("tm")
    band_groups = lax.axis_size("band")
    taps_count, channels = taps.shape
    _, inputs, samples = volts.shape
    reach = taps_count * channels
    history = lax.ppermute(volts[:, :, samples - reach :], "tm", [(i, i + 1) for i in range(time_groups - 1)])
    spectra = channelize(volts, history, taps)
    turned = lax.all_to_all(spectra, ("tm", "band"), split_axis=0, concat_axis=0, tiled=True)
    return correlate(turned.reshape(time_groups, band_groups, 2, inputs, samples // channels))


def solution(mesh):
    in_specs = (P(None, "band", "tm"), P())
    out_specs = P(("tm", "band"), None, None, None)
    return jax.shard_map(
        per_device, mesh=mesh, in_specs=in_specs, out_specs=out_specs, check_vma=False
    )
```
